256 devices in a mesh: layer: 8 (over y, core), row: 32 (over x, z).
Axes of the slice: x: 4, y: 4, z: 8, core: 2. Of those that a mesh axis runs over, the one named last changes fastest.
Arguments:
- transmission: bfloat16 [8, 6144, 6144], P('layer', 'row'), may hold values from -0.078125 to 0.078125
- reflection: bfloat16 [8, 6144, 6144], P('layer', 'row'), may hold values from -0.078125 to 0.078125
- receiver_map: bfloat16 [8, 6144, 6144], P('layer', 'row'), may hold values from -0.078125 to 0.078125
- midplane_map: bfloat16 [8, 6144, 6144], P('layer', 'row'), may hold values from -0.078125 to 0.078125
- traces: bfloat16 [8, 6144, 384], P('layer', 'row'), may hold values from -6 to 6
- sources: bfloat16 [8, 3, 6144, 384], P('layer', None, 'row'), may hold values from -5 to 5
Outputs:
- reflected: bfloat16 [8, 3, 6144, 384], P('layer', None, 'row')
- recorded: bfloat16 [8, 3, 6144, 384], P('layer', None, 'row')
- midfield: bfloat16 [8, 3, 6144, 384], P('layer', None, 'row')
- transmitted: bfloat16 [8, 6144, 384], P('layer', 'row')
The draws below stay inside these ranges and needn't reach their ends.
All inputs are finite; a program needn't handle non-finite values.
Results may differ from the reference program's by a relative error of at most 0.0052.
Values may be sent and summed in bfloat16 or wider, within the bound.
A program may use at most 128 MiB of HBM per device.

```python
import jax
import jax.numpy as jnp
from jax import lax

M = 6144
B = 384
TICKS = 3
SECTIONS = 8


def level_of(own_key, shape, shards, smallest, top_value):
    gain, own = 1.0, jax.random.fold_in(own_key, 6)
    for position, parts in shards:
        steps = jnp.exp(jax.random.uniform(jax.random.fold_in(own, position), (parts,), jnp.float32, smallest / len(shards), top_value / len(shards)))
        gain = gain * jnp.repeat(steps, shape[position] // parts).reshape([-1 if axis == position else 1 for axis in range(len(shape))])
    return gain


def bell_draw(rng, extent, width, bound, shards=(), kind=jnp.bfloat16):
    drawn = jax.random.normal(rng, extent, jnp.float32) * width
    if len(shards) > 0:
        drawn = level_of(rng, extent, shards, -0.22, 0.18) * drawn
    return jnp.clip(drawn, min=-bound, max=bound).astype(kind)


def setup_inputs(seed: int = 0) -> dict:
    arg_keys = jax.random.split(jax.random.key(seed), 7)
    transmission = bell_draw(arg_keys[0], (SECTIONS, M, M), M ** -0.5, 0.078125, ((0, 8), (1, 32)))
    reflection = bell_draw(arg_keys[1], (SECTIONS, M, M), M ** -0.5, 0.078125, ((0, 8), (1, 32)))
    receiver_map = bell_draw(arg_keys[2], (SECTIONS, M, M), M ** -0.5, 0.078125, ((0, 8), (1, 32)))
    midplane_map = bell_draw(arg_keys[3], (SECTIONS, M, M), M ** -0.5, 0.078125, ((0, 8), (1, 32)))
    traces = bell_draw(arg_keys[4], (SECTIONS, M, B), 1.0, 6.0, ((0, 8), (1, 32)))
    sources = bell_draw(arg_keys[5], (SECTIONS, TICKS, M, B), 0.7, 5.0, ((0, 8), (2, 32)))
    return dict(transmission=transmission, reflection=reflection, receiver_map=receiver_map, midplane_map=midplane_map, traces=traces, sources=sources)


def one_section(operands):
    transmit_rows, reflect_rows, receive_rows, middle_rows, incoming, source_now = operands
    sent = jnp.dot(transmit_rows, incoming, preferred_element_type=jnp.float32) + source_now.astype(jnp.float32)
    bounced = jnp.dot(reflect_rows, incoming, preferred_element_type=jnp.float32)
    heard = jnp.dot(receive_rows, incoming, preferred_element_type=jnp.float32)
    middle = jnp.dot(middle_rows, incoming, preferred_element_type=jnp.float32)
    return (sent.astype(jnp.bfloat16), bounced.astype(jnp.bfloat16),
            heard.astype(jnp.bfloat16), middle.astype(jnp.bfloat16))


def reference(transmission, reflection, receiver_map, midplane_map, traces, sources):
    incoming = traces
    bounced_all = []
    heard_all = []
    middle_all = []
    sent = traces
    for tick in range(TICKS):
        sent, bounced, heard, middle = lax.map(one_section, (transmission, reflection, receiver_map, midplane_map, incoming, sources[:, tick]))
        bounced_all.append(bounced)
        heard_all.append(heard)
        middle_all.append(middle)
        incoming = jnp.concatenate([jnp.zeros((1, M, B), jnp.bfloat16), sent[:-1]], axis=0)
    return (jnp.stack(bounced_all, axis=1), jnp.stack(heard_all, axis=1),
            jnp.stack(middle_all, axis=1), sent)
```

```python
import functools

import jax
import jax.numpy as jnp
from jax import lax
from jax.experimental import pallas as pl
from jax.experimental.pallas import tpu as pltpu
from jax.sharding import PartitionSpec as P

MESH = pl.DeviceIdType.MESH

TICKS = 3
LAYERS = 8
XS, ZS = 4, 8
ROWS = 192
M = XS * ZS * ROWS
B = 384
WIDE = 128
STREAMS = B // WIDE
UNITS = TICKS * STREAMS

SPLITS = (
    ((0, 32, 1), (32, 48, -1), (80, 64, 1), (144, 48, -1)),
    ((0, 48, 1), (48, 32, -1), (80, 48, 1), (128, 64, -1)),
)
HOPS = XS - 1 + ZS - 1
ROUNDS = XS // 2 + ZS // 2 + 1


def hops_of(length):
    found = []
    for hop in range(1, length // 2 + 1):
        found.append((True, hop))
        if hop < length // 2:
            found.append((False, hop))
    return found


def slot_order():
    order = []
    period, shift = ROUNDS + 2, 3
    last = period * TICKS + shift * STREAMS + 8
    for slot in range(last):
        for c in range(STREAMS):
            for t in range(TICKS):
                r = slot - shift * c - period * t
                if 0 <= r <= ROUNDS:
                    order.append((t, c, r))
                elif ROUNDS < r <= ROUNDS + 3:
                    order.append((t, c, r))
    return order


def kernel(
    trans_hbm, refl_hbm, recv_hbm, mid_hbm, traces_hbm, sources_hbm,
    bounced_hbm, heard_hbm, middle_hbm, trans_out_hbm,
    a_v, g, src_v, sent_v, out_v,
    send_sem, recv_sem, pd_send, pd_recv, in_sem, tr_sem, src_sem, out_sem,
):
    layer = lax.axis_index("layer")
    row = lax.axis_index("row")
    x, z = row // ZS, row % ZS

    mats = (trans_hbm, refl_hbm, recv_hbm, mid_hbm)
    outs = (trans_out_hbm, bounced_hbm, heard_hbm, middle_hbm)

    def trace_copy(c):
        return pltpu.make_async_copy(
            traces_hbm.at[:, pl.ds(c * WIDE, WIDE)], g.at[c, x, z], tr_sem.at[c]
        )

    def mat_copy(j):
        return pltpu.make_async_copy(mats[j], a_v.at[j], in_sem.at[j])

    source_copy = pltpu.make_async_copy(sources_hbm, src_v, src_sem)

    for c in range(STREAMS):
        trace_copy(c).start()
    for j in range(4):
        mat_copy(j).start()
    source_copy.start()

    def at_x(k):
        return lax.rem(x + (k + XS), XS)

    def at_z(k):
        return lax.rem(z + (k + ZS), ZS)

    barrier = pltpu.get_barrier_semaphore()
    around = [(at_x(1), z), (at_x(-1), z), (x, at_z(1)), (x, at_z(-1))]
    for nx, nz in around:
        pl.semaphore_signal(barrier, inc=1, device_id=(layer, nx * ZS + nz), device_id_type=MESH)

    @pl.when(layer < LAYERS - 1)
    def _():
        pl.semaphore_signal(barrier, inc=1, device_id=(layer + 1, row), device_id_type=MESH)

    @pl.when(layer > 0)
    def _():
        pl.semaphore_signal(barrier, inc=1, device_id=(layer - 1, row), device_id_type=MESH)

    ends = jnp.where(layer > 0, 1, 0) + jnp.where(layer < LAYERS - 1, 1, 0)
    pl.semaphore_wait(barrier, len(around) + ends)

    def region(u, part, first, axis, back):
        start, size, _ = part
        rows = pl.ds(start, size)
        if first:
            if axis == "x":
                return g.at[u, at_x(-back), z, rows]
            return g.at[u, x, at_z(-back), rows]
        if axis == "x":
            return g.at[u, at_x(-back), :, rows]
        return g.at[u, :, at_z(-back), rows]

    started = []

    def moves(u, index):
        part = SPLITS[u % 2][index]
        axes = (("x", XS), ("z", ZS)) if index < 2 else (("z", ZS), ("x", XS))
        listed = []
        base, number = 0, 0
        for phase, (axis, length) in enumerate(axes):
            for long_way, hop in hops_of(length):
                way = part[2] if long_way else -part[2]
                if axis == "x":
                    target = (layer, at_x(way) * ZS + z)
                else:
                    target = (layer, x * ZS + at_z(way))
                slot = index * HOPS + number
                number += 1

                def copy(back, phase=phase, axis=axis, target=target, slot=slot):
                    moved = region(u, part, phase == 0, axis, back)
                    return pltpu.make_async_remote_copy(
                        src_ref=moved,
                        dst_ref=moved,
                        send_sem=send_sem.at[u, slot],
                        recv_sem=recv_sem.at[u, slot],
                        device_id=target,
                        device_id_type=MESH,
                    )

                listed.append((base + hop - 1, "send", functools.partial(copy, way * (hop - 1))))
                listed.append((base + hop, "recv", functools.partial(copy, way * hop)))
            base += length // 2
        return listed

    def down(u):
        return pltpu.make_async_remote_copy(
            src_ref=sent_v.at[u],
            dst_ref=g.at[u + STREAMS, x, z],
            send_sem=pd_send.at[u],
            recv_sem=pd_recv.at[u],
            device_id=(lax.rem(layer + 1, LAYERS), row),
            device_id_type=MESH,
        )

    def dot(j, u):
        data = g[u].reshape(M, WIDE)
        return jnp.dot(a_v[j], data, preferred_element_type=jnp.float32)

    out_copies = []

    def put(j, t, c):
        columns = pl.ds(c * WIDE, WIDE)
        if j == 0:
            src, dst = out_v.at[0, :, columns], outs[0].at[:, columns]
        else:
            place = 1 + (j - 1) * TICKS + t
            src, dst = out_v.at[place, :, columns], outs[j].at[t, :, columns]
        copy = pltpu.make_async_copy(src, dst, out_sem.at[len(out_copies)])
        copy.start()
        out_copies.append(copy)

    waited = set()

    def need(j):
        if j not in waited:
            waited.add(j)
            mat_copy(j).wait()

    def step(t, c, r):
        u = t * STREAMS + c
        if r == 0:
            if t == 0:
                trace_copy(c).wait()
            else:
                @pl.when(layer > 0)
                def _():
                    down(u - STREAMS).wait_recv()

                @pl.when(layer == 0)
                def _():
                    g[u, x, z] = jnp.zeros((ROWS, WIDE), jnp.bfloat16)
        if r < ROUNDS:
            parts = [moves(u, index) for index in range(4)]
            for listed in parts:
                for when, kind, copy in listed:
                    if when == r and kind == "recv":
                        copy().wait_recv()
                for when, kind, copy in listed:
                    if when == r and kind == "send":
                        sending = copy()
                        sending.start()
                        started.append(sending)
        elif r == ROUNDS:
            need(0)
            if "s" not in waited:
                waited.add("s")
                source_copy.wait()
            columns = pl.ds(c * WIDE, WIDE)
            sent = dot(0, u) + src_v[t, :, columns].astype(jnp.float32)
            sent = sent.astype(jnp.bfloat16)
            if t + 1 < TICKS:
                sent_v[u] = sent

                @pl.when(layer < LAYERS - 1)
                def _():
                    down(u).start()
            else:
                out_v[0, :, columns] = sent
                put(0, t, c)
        else:
            j = r - ROUNDS
            need(j)
            place = 1 + (j - 1) * TICKS + t
            out_v[place, :, pl.ds(c * WIDE, WIDE)] = dot(j, u).astype(jnp.bfloat16)
            put(j, t, c)

    for t, c, r in slot_order():
        step(t, c, r)

    for copy in started:
        copy.wait_send()

    @pl.when(layer < LAYERS - 1)
    def _():
        for u in range(UNITS - STREAMS):
            down(u).wait_send()

    for copy in out_copies:
        copy.wait()


def shards(transmission, reflection, receiver_map, midplane_map, traces, sources):
    stacked = jax.ShapeDtypeStruct((TICKS, ROWS, B), jnp.bfloat16)
    n_outs = (TICKS * 3 + 1) * STREAMS
    results = pl.pallas_call(
        kernel,
        out_shape=(stacked, stacked, stacked, jax.ShapeDtypeStruct((ROWS, B), jnp.bfloat16)),
        in_specs=[pl.BlockSpec(memory_space=pl.ANY)] * 6,
        out_specs=[pl.BlockSpec(memory_space=pl.ANY)] * 4,
        scratch_shapes=[
            pltpu.VMEM((4, ROWS, M), jnp.bfloat16),
            pltpu.VMEM((UNITS, XS, ZS, ROWS, WIDE), jnp.bfloat16),
            pltpu.VMEM((TICKS, ROWS, B), jnp.bfloat16),
            pltpu.VMEM((UNITS - STREAMS, ROWS, WIDE), jnp.bfloat16),
            pltpu.VMEM((1 + 3 * TICKS, ROWS, B), jnp.bfloat16),
            pltpu.SemaphoreType.DMA((UNITS, 4 * HOPS)),
            pltpu.SemaphoreType.DMA((UNITS, 4 * HOPS)),
            pltpu.SemaphoreType.DMA((UNITS - STREAMS,)),
            pltpu.SemaphoreType.DMA((UNITS - STREAMS,)),
            pltpu.SemaphoreType.DMA((4,)),
            pltpu.SemaphoreType.DMA((STREAMS,)),
            pltpu.SemaphoreType.DMA,
            pltpu.SemaphoreType.DMA((n_outs,)),
        ],
        compiler_params=pltpu.CompilerParams(
            collective_id=0, has_side_effects=True, vmem_limit_bytes=48 * 1024 * 1024
        ),
    )(transmission[0], reflection[0], receiver_map[0], midplane_map[0], traces[0], sources[0])
    bounced, heard, middle, sent = results
    return bounced[None], heard[None], middle[None], sent[None]


def solution(mesh):
    return jax.shard_map(
        shards,
        mesh=mesh,
        in_specs=(
            P("layer", "row", None),
            P("layer", "row", None),
            P("layer", "row", None),
            P("layer", "row", None),
            P("layer", "row", None),
            P("layer", None, "row", None),
        ),
        out_specs=(
            P("layer", None, "row", None),
            P("layer", None, "row", None),
            P("layer", None, "row", None),
            P("layer", "row", None),
        ),
        check_vma=False,
    )
```

```python
import functools

import jax
import jax.numpy as jnp
from jax import lax
from jax.experimental import pallas as pl
from jax.experimental.pallas import tpu as pltpu
from jax.sharding import PartitionSpec as P

MESH = pl.DeviceIdType.MESH

TICKS = 3
LAYERS = 8
XS, ZS = 4, 8
ROWS = 192
M = XS * ZS * ROWS
B = 384
WIDE = 128
STREAMS = B // WIDE
UNITS = TICKS * STREAMS

SPLITS = (((0, 32, 1), (32, 48, -1), (80, 64, 1), (144, 48, -1)), ((0, 48, 1), (48, 32, -1), (80, 48, 1), (128, 64, -1)))
X_FIRST = ((0, 1), (0, -1), (0, 2))
X_SECOND = ((0, 1), (0, -1), (1, 2))
Z_FIRST = ((0, 1), (0, -1), (1, 2), (-1, -2), (2, 3), (-2, -3), (3, 4))
Z_SECOND = ((0, 1), (0, -1), (1, 2), (-1, -2), (2, 3), (-2, -3), (3, 4))
X_GROUPS = ((0, 1, -1, 2),)
Z_GROUPS = ((0, 1, -1), (2, -2, 3, -3, 4))

ORDER = (
    90, 0, 1, 10, 33, 34, 11, 21, 20, 2, 12, 35, 36, 23, 40, 41, 22, 190, 4, 3, 28, 27, 13, 14, 37, 38, 25, 24, 111,
    42, 110, 100, 120, 121, 134, 133, 101, 112, 5, 6, 102, 29, 16, 15, 39, 26, 122, 123, 136, 127, 128, 135, 290, 114,
    113, 141, 140, 7, 8, 103, 104, 43, 44, 18, 17, 124, 125, 138, 137, 234, 233, 31, 30, 220, 201, 221, 116, 115, 129,
    210, 200, 9, 212, 211, 106, 142, 202, 105, 126, 19, 236, 45, 139, 241, 222, 235, 240, 223, 118, 117, 228, 32, 91,
    214, 213, 203, 227, 108, 131, 107, 204, 238, 130, 237, 224, 225, 92, 119, 143, 390, 144, 242, 216, 215, 93, 229,
    205, 206, 239, 109, 132, 226, 311, 300, 320, 321, 334, 333, 302, 145, 191, 218, 217, 310, 301, 207, 208, 312, 94,
    322, 244, 243, 323, 336, 335, 192, 230, 231, 490, 219, 327, 328, 303, 193, 209, 304, 341, 340, 314, 313, 324, 325,
    338, 337, 245, 401, 433, 434, 410, 421, 420, 232, 291, 305, 412, 400, 411, 306, 316, 342, 402, 326, 329, 315, 339,
    436, 435, 440, 441, 423, 422, 194, 428, 427, 590, 307, 413, 292, 414, 330, 308, 331, 318, 404, 293, 317, 403, 438,
    344, 437, 424, 343, 425, 520, 521, 442, 429, 534, 533, 510, 511, 500, 501, 309, 415, 512, 502, 406, 416, 332, 319,
    405, 439, 426, 523, 527, 345, 391, 522, 535, 417, 536, 541, 514, 528, 513, 503, 540, 294, 504, 418, 443, 444, 408,
    407, 525, 524, 537, 690, 538, 516, 431, 430, 419, 392, 515, 529, 505, 542, 393, 506, 409, 600, 539, 445, 526, 633,
    634, 518, 611, 601, 621, 620, 610, 602, 612, 517, 432, 491, 507, 508, 394, 635, 636, 543, 544, 623, 622, 492, 604,
    603, 531, 530, 790, 613, 640, 614, 519, 641, 637, 628, 509, 625, 627, 638, 624, 493, 606, 605, 545, 710, 720, 721,
    734, 733, 532, 591, 642, 616, 615, 701, 639, 626, 711, 712, 700, 629, 608, 607, 702, 722, 723, 736, 727, 728, 735,
    494, 741, 890, 740, 618, 617, 592, 643, 644, 713, 714, 609, 704, 725, 631, 737, 630, 703, 724, 801, 833, 810, 821,
    738, 729, 834, 800, 820, 619, 812, 811, 742, 802, 716, 715, 593, 645, 706, 739, 705, 835, 726, 632, 691, 840, 823,
    836, 822, 841, 813, 828, 814, 804, 827, 803, 717, 718, 594, 708, 837, 743, 707, 744, 838, 825, 824, 692, 731, 730,
    815, 816, 842, 806, 805, 829, 719, 839, 709, 826, 745, 693, 817, 818, 732, 791, 808, 807, 694, 843, 844, 792, 793,
    831, 830, 819, 809, 794, 845, 832, 891, 892, 893, 894,
)

def copies_of(u):
    found = []
    for part in range(4):
        first, second, groups = (X_FIRST, Z_SECOND, X_GROUPS) if part < 2 else (Z_FIRST, X_SECOND, Z_GROUPS)
        for back, to in first:
            found.append((part, 0, None, back, to))
        for group in range(len(groups)):
            for back, to in second:
                found.append((part, 1, group, back, to))
    return found


def needs_of(copy):
    part, phase, group, back, _ = copy
    if phase == 0:
        return [] if back == 0 else [(part, 0, None, back)]
    if back != 0:
        return [(part, 1, group, back)]
    groups = X_GROUPS if part < 2 else Z_GROUPS
    return [(part, 0, None, away) for away in groups[group] if away != 0]


COPIES = copies_of(0)


def size_of(u, copy):
    part, phase, group, _, _ = copy
    groups = X_GROUPS if part < 2 else Z_GROUPS
    return SPLITS[u % len(SPLITS)][part][1] * (len(groups[group]) if phase else 1)


def send_key(u, copy):
    rows, phase, far = size_of(u, copy), copy[1], abs(copy[4] - copy[3])
    return (-phase, rows)


def kernel(
    trans_hbm, refl_hbm, recv_hbm, mid_hbm, traces_hbm, sources_hbm,
    bounced_hbm, heard_hbm, middle_hbm, trans_out_hbm,
    a_v, g, src_v, sent_v, out_v,
    send_sem, recv_sem, pd_send, pd_recv, in_sem, tr_sem, src_sem, out_sem,
):
    layer = lax.axis_index("layer")
    row = lax.axis_index("row")
    x, z = row // ZS, row % ZS

    mats = (trans_hbm, refl_hbm, recv_hbm, mid_hbm)
    outs = (trans_out_hbm, bounced_hbm, heard_hbm, middle_hbm)

    def trace_copy(c):
        return pltpu.make_async_copy(
            traces_hbm.at[:, pl.ds(c * WIDE, WIDE)], g.at[c, x, z], tr_sem.at[c]
        )

    def mat_copy(j):
        return pltpu.make_async_copy(mats[j], a_v.at[j], in_sem.at[j])

    source_copy = pltpu.make_async_copy(sources_hbm, src_v, src_sem)

    for c in range(STREAMS):
        trace_copy(c).start()
    for j in range(4):
        mat_copy(j).start()
    source_copy.start()

    xs = {k: lax.rem(x + (k + XS), XS) for k in range(-2, 3)}
    zs = {k: lax.rem(z + (k + ZS), ZS) for k in range(-4, 5)}
    x_devices = {k: xs[k] * ZS + z for k in range(-2, 3)}
    z_devices = {k: x * ZS + zs[k] for k in range(-4, 5)}

    reach_x = sorted({(way * (to - back)) % XS for back, to in X_FIRST + X_SECOND for way in (1, -1)})
    reach_z = sorted({(way * (to - back)) % ZS for back, to in Z_FIRST + Z_SECOND for way in (1, -1)})
    around = [xs[k if k <= 2 else k - XS] * ZS + z for k in reach_x]
    around += [x * ZS + zs[k if k <= 4 else k - ZS] for k in reach_z]

    barrier = pltpu.get_barrier_semaphore()
    for other in around:
        pl.semaphore_signal(barrier, inc=1, device_id=(layer, other), device_id_type=MESH)

    @pl.when(layer < LAYERS - 1)
    def _():
        pl.semaphore_signal(barrier, inc=1, device_id=(layer + 1, row), device_id_type=MESH)

    @pl.when(layer > 0)
    def _():
        pl.semaphore_signal(barrier, inc=1, device_id=(layer - 1, row), device_id_type=MESH)

    ends = jnp.where(layer > 0, 1, 0) + jnp.where(layer < LAYERS - 1, 1, 0)
    pl.semaphore_wait(barrier, len(around) + ends)

    def regions(u, copy, distance):
        part, phase, group, _, _ = copy
        start, size, way = SPLITS[u % len(SPLITS)][part]
        rows = pl.ds(start, size)
        along_x = (part < 2) == (phase == 0)
        if along_x:
            here = xs[-way * distance]
            if phase == 0:
                return [g.at[u, here, z, rows]]
            if len(Z_GROUPS[group]) == ZS:
                return [g.at[u, here, :, rows]]
            return [g.at[u, here, zs[-way * away], rows] for away in Z_GROUPS[group]]
        here = zs[-way * distance]
        if phase == 0:
            return [g.at[u, x, here, rows]]
        if len(X_GROUPS[group]) == XS:
            return [g.at[u, :, here, rows]]
        return [g.at[u, xs[-way * away], here, rows] for away in X_GROUPS[group]]

    def send(u, number):
        copy = COPIES[number]
        part, phase, _, back, to = copy
        way = SPLITS[u % len(SPLITS)][part][2]
        along_x = (part < 2) == (phase == 0)
        target = (x_devices if along_x else z_devices)[way * (to - back)]
        for moved in regions(u, copy, back):
            pltpu.make_async_remote_copy(
                src_ref=moved,
                dst_ref=moved,
                send_sem=send_sem.at[u],
                recv_sem=recv_sem.at[u, number],
                device_id=(layer, target),
                device_id_type=MESH,
            ).start()

    def receive(u, number):
        copy = COPIES[number]
        part, phase, group, _, to = copy
        moved = regions(u, copy, to)
        if len(moved) == 1:
            whole = moved[0]
        else:
            start, size, _ = SPLITS[u % len(SPLITS)][part]
            rows = pl.ds(start, size)
            whole = g.at[u, pl.ds(0, len(moved)), 0, rows] if part < 2 else g.at[u, 0, pl.ds(0, len(moved)), rows]
        pltpu.make_async_copy(whole, whole, recv_sem.at[u, number]).wait()

    def all_sent(u):
        whole = g.at[u].reshape(XS * ZS, ROWS, WIDE).at[pl.ds(0, XS * ZS - 1)]
        pltpu.make_async_copy(whole, whole, send_sem.at[u]).wait()

    def down(u):
        return pltpu.make_async_remote_copy(
            src_ref=sent_v.at[u],
            dst_ref=g.at[u + STREAMS, x, z],
            send_sem=pd_send.at[u],
            recv_sem=pd_recv.at[u],
            device_id=(lax.rem(layer + 1, LAYERS), row),
            device_id_type=MESH,
        )

    def dot(j, u):
        data = g[u].reshape(M, WIDE)
        return jnp.dot(a_v[j], data, preferred_element_type=jnp.float32)

    out_copies = []

    def put(j, t, c):
        columns = pl.ds(c * WIDE, WIDE)
        if j == 0:
            src, dst = out_v.at[0, :, columns], outs[0].at[:, columns]
        else:
            place = 1 + (j - 1) * TICKS + t
            src, dst = out_v.at[place, :, columns], outs[j].at[t, :, columns]
        copy = pltpu.make_async_copy(src, dst, out_sem.at[len(out_copies)])
        copy.start()
        out_copies.append(copy)

    waited = set()

    def need(j):
        if j not in waited:
            waited.add(j)
            if j == "sources":
                source_copy.wait()
            else:
                mat_copy(j).wait()

    here = {u: set() for u in range(UNITS)}
    gone = {u: set() for u in range(UNITS)}

    def send_ready(u):
        ready = [
            n
            for n, copy in enumerate(COPIES)
            if n not in gone[u] and all(needed in here[u] for needed in needs_of(copy))
        ]
        for n in sorted(ready, key=lambda n: send_key(u, COPIES[n])):
            gone[u].add(n)
            send(u, n)

    def begin(t, c, u):
        if t == 0:
            trace_copy(c).wait()
        else:

            @pl.when(layer > 0)
            def _():
                down(u - STREAMS).wait_recv()

            @pl.when(layer == 0)
            def _():
                g[u, x, z] = jnp.zeros((ROWS, WIDE), jnp.bfloat16)

        send_ready(u)

    def transmit(t, c, u):
        need(0)
        need("sources")
        columns = pl.ds(c * WIDE, WIDE)
        sent = dot(0, u) + src_v[t, :, columns].astype(jnp.float32)
        sent = sent.astype(jnp.bfloat16)
        if t + 1 < TICKS:
            sent_v[u] = sent

            @pl.when(layer < LAYERS - 1)
            def _():
                down(u).start()
        else:
            out_v[0, :, columns] = sent
            put(0, t, c)

    for task in ORDER:
        u, n = divmod(task, 100)
        t, c = divmod(u, STREAMS)
        if n == 90:
            begin(t, c, u)
        elif n == 91:
            transmit(t, c, u)
        elif n > 91:
            j = n - 91
            need(j)
            place = 1 + (j - 1) * TICKS + t
            out_v[place, :, pl.ds(c * WIDE, WIDE)] = dot(j, u).astype(jnp.bfloat16)
            put(j, t, c)
        else:
            receive(u, n)
            part, phase, group, _, to = COPIES[n]
            here[u].add((part, phase, group, to))
            send_ready(u)

    for u in range(UNITS):
        all_sent(u)

    @pl.when(layer < LAYERS - 1)
    def _():
        for u in range(UNITS - STREAMS):
            down(u).wait_send()

    for copy in out_copies:
        copy.wait()


def shards(transmission, reflection, receiver_map, midplane_map, traces, sources):
    stacked = jax.ShapeDtypeStruct((TICKS, ROWS, B), jnp.bfloat16)
    n_outs = (TICKS * 3 + 1) * STREAMS
    results = pl.pallas_call(
        kernel,
        out_shape=(stacked, stacked, stacked, jax.ShapeDtypeStruct((ROWS, B), jnp.bfloat16)),
        in_specs=[pl.BlockSpec(memory_space=pl.ANY)] * 6,
        out_specs=[pl.BlockSpec(memory_space=pl.ANY)] * 4,
        scratch_shapes=[
            pltpu.VMEM((4, ROWS, M), jnp.bfloat16),
            pltpu.VMEM((UNITS, XS, ZS, ROWS, WIDE), jnp.bfloat16),
            pltpu.VMEM((TICKS, ROWS, B), jnp.bfloat16),
            pltpu.VMEM((UNITS - STREAMS, ROWS, WIDE), jnp.bfloat16),
            pltpu.VMEM((1 + 3 * TICKS, ROWS, B), jnp.bfloat16),
            pltpu.SemaphoreType.DMA((UNITS,)),
            pltpu.SemaphoreType.DMA((UNITS, len(COPIES))),
            pltpu.SemaphoreType.DMA((UNITS - STREAMS,)),
            pltpu.SemaphoreType.DMA((UNITS - STREAMS,)),
            pltpu.SemaphoreType.DMA((4,)),
            pltpu.SemaphoreType.DMA((STREAMS,)),
            pltpu.SemaphoreType.DMA,
            pltpu.SemaphoreType.DMA((n_outs,)),
        ],
        compiler_params=pltpu.CompilerParams(
            collective_id=0, has_side_effects=True, vmem_limit_bytes=48 * 1024 * 1024
        ),
    )(transmission[0], reflection[0], receiver_map[0], midplane_map[0], traces[0], sources[0])
    bounced, heard, middle, sent = results
    return bounced[None], heard[None], middle[None], sent[None]


def solution(mesh):
    return jax.shard_map(
        shards,
        mesh=mesh,
        in_specs=(
            P("layer", "row", None),
            P("layer", "row", None),
            P("layer", "row", None),
            P("layer", "row", None),
            P("layer", "row", None),
            P("layer", None, "row", None),
        ),
        out_specs=(
            P("layer", None, "row", None),
            P("layer", None, "row", None),
            P("layer", None, "row", None),
            P("layer", "row", None),
        ),
        check_vma=False,
    )
```

```python
import functools

import jax
import jax.numpy as jnp
from jax import lax
from jax.experimental import pallas as pl
from jax.experimental.pallas import tpu as pltpu
from jax.sharding import PartitionSpec as P

MESH = pl.DeviceIdType.MESH

TICKS = 3
LAYERS = 8
XS, ZS = 4, 8
ROWS = 192
M = XS * ZS * ROWS
B = 384
WIDE = 128
STREAMS = B // WIDE
VMEM = 62 * 1024 * 1024
UNITS = TICKS * STREAMS

SPLITS = (
    ((0, 32, 1), (32, 32, -1), (64, 64, 1), (128, 64, -1)),
    ((0, 32, 1), (32, 48, -1), (80, 64, 1), (144, 48, -1)),
    ((0, 48, 1), (48, 48, -1), (96, 48, 1), (144, 48, -1)),
    ((0, 32, 1), (32, 32, -1), (64, 64, -1), (128, 64, 1)),
    ((0, 16, 1), (16, 32, -1), (48, 64, 1), (112, 80, -1)),
    ((0, 32, 1), (32, 16, -1), (48, 80, 1), (128, 64, -1)),
)
X_TREES = (
    ((0, 1), (0, -1), (1, 2)),
    ((0, 1), (0, -1), (0, 2)),
)
Z_TREES = (
    ((0, 1), (0, -1), (1, 2), (-1, -2), (2, 3), (-2, -3), (3, 4)),
    ((0, 1), (0, -1), (0, 2), (0, -2), (2, 3), (-2, -3), (3, 4)),
    ((0, 1), (0, -1), (0, 2), (0, -2), (2, 3), (-2, -3), (2, 4)),
    ((0, 1), (0, -1), (0, 2), (0, -2), (0, 3), (0, -3), (0, 4)),
)
PLANS = (
    (5, 1, 0, 2, 0),
    (2, 1, 0, 0, 0),
    (3, 0, 0, 0, 0),
    (4, 1, 0, 2, 0),
    (4, 1, 0, 2, 0),
    (2, 1, 0, 1, 0),
    (0, 1, 1, 1, 0),
    (1, 1, 0, 2, 0),
    (2, 1, 0, 2, 0),
)
X_GROUPS = ((0, 1, -1, 2),)
Z_GROUPS = ((0, 1, -1), (2, -2, 3, -3, 4))

ORDER = (
    90, 290, 10, 11, 1, 0, 12, 190, 2, 35, 36, 33, 34, 23, 22, 21, 20, 200, 201, 220, 221, 211, 210, 234, 13, 14, 233,
    120, 121, 100, 101, 3, 4, 102, 38, 111, 110, 112, 134, 40, 41, 133, 37, 39, 222, 223, 25, 24, 26, 202, 16, 15,
    236, 212, 235, 123, 122, 227, 228, 28, 27, 241, 6, 240, 5, 104, 103, 128, 127, 113, 114, 135, 136, 141, 42, 224,
    225, 140, 204, 203, 17, 18, 238, 44, 214, 213, 237, 125, 124, 43, 8, 7, 30, 106, 105, 31, 29, 115, 116, 137, 138,
    229, 226, 242, 205, 206, 142, 19, 216, 129, 239, 215, 126, 45, 9, 108, 32, 91, 117, 107, 139, 230, 231, 208, 118,
    207, 217, 92, 218, 244, 243, 390, 119, 131, 130, 109, 209, 219, 143, 144, 93, 94, 232, 301, 322, 245, 291, 323,
    320, 321, 300, 302, 310, 312, 311, 132, 336, 145, 191, 335, 334, 333, 292, 324, 325, 326, 303, 304, 590, 314, 313,
    338, 327, 490, 328, 337, 339, 340, 341, 305, 306, 293, 522, 523, 331, 330, 520, 521, 534, 501, 500, 536, 316, 315,
    502, 510, 511, 401, 512, 410, 533, 412, 329, 422, 423, 400, 411, 535, 402, 420, 421, 436, 435, 434, 433, 343, 307,
    308, 524, 525, 538, 344, 317, 318, 342, 294, 504, 528, 503, 192, 332, 540, 513, 514, 425, 527, 193, 424, 413, 428,
    426, 414, 404, 541, 440, 427, 403, 438, 537, 437, 309, 439, 441, 319, 526, 529, 505, 345, 391, 542, 506, 516, 194,
    416, 430, 415, 405, 515, 406, 431, 539, 429, 392, 442, 507, 690, 508, 518, 444, 393, 418, 417, 407, 443, 530, 517,
    408, 394, 531, 509, 432, 623, 543, 621, 635, 622, 601, 633, 610, 544, 620, 612, 600, 636, 611, 602, 634, 419, 409,
    519, 532, 625, 445, 491, 637, 624, 492, 545, 591, 638, 627, 628, 493, 641, 615, 613, 640, 616, 614, 790, 494, 606,
    890, 626, 639, 617, 618, 642, 629, 604, 605, 603, 700, 702, 711, 735, 701, 736, 710, 733, 712, 723, 721, 734, 722,
    720, 608, 800, 801, 802, 811, 810, 822, 812, 820, 823, 834, 836, 821, 630, 631, 607, 833, 619, 835, 703, 738, 737,
    592, 644, 643, 714, 739, 741, 740, 724, 713, 704, 725, 726, 727, 728, 827, 828, 803, 804, 824, 840, 826, 813, 825,
    632, 814, 838, 837, 593, 645, 609, 691, 715, 841, 705, 744, 839, 743, 742, 716, 706, 806, 594, 730, 815, 805, 731,
    816, 729, 692, 842, 707, 717, 829, 693, 708, 831, 718, 830, 694, 808, 843, 844, 807, 817, 818, 745, 719, 709, 732,
    791, 792, 832, 793, 794, 845, 819, 809, 891, 892, 893, 894,
)

def copies_of(u):
    found = []
    _, x_first, z_second, z_first, x_second = PLANS[u]
    for part in range(4):
        first, second, groups = (
            (X_TREES[x_first], Z_TREES[z_second], X_GROUPS) if part < 2 else (Z_TREES[z_first], X_TREES[x_second], Z_GROUPS)
        )
        for back, to in first:
            found.append((part, 0, None, back, to))
        for group in range(len(groups)):
            for back, to in second:
                found.append((part, 1, group, back, to))
    return found


def needs_of(copy):
    part, phase, group, back, _ = copy
    if phase == 0:
        return [] if back == 0 else [(part, 0, None, back)]
    if back != 0:
        return [(part, 1, group, back)]
    groups = X_GROUPS if part < 2 else Z_GROUPS
    return [(part, 0, None, away) for away in groups[group] if away != 0]


COPIES = [copies_of(u) for u in range(UNITS)]


def split_of(u):
    return SPLITS[PLANS[u][0]]


def size_of(u, copy):
    part, phase, group, _, _ = copy
    groups = X_GROUPS if part < 2 else Z_GROUPS
    return split_of(u)[part][1] * (len(groups[group]) if phase else 1)


def send_key(u, copy):
    rows, phase, far = size_of(u, copy), copy[1], abs(copy[4] - copy[3])
    return (phase, -far, rows)


def kernel(
    trans_hbm, refl_hbm, recv_hbm, mid_hbm, traces_hbm, sources_hbm,
    bounced_hbm, heard_hbm, middle_hbm, trans_out_hbm,
    a_v, g, src_v, sent_v, out_v,
    send_sem, recv_sem, pd_send, pd_recv, in_sem, tr_sem, src_sem, out_sem,
):
    layer = lax.axis_index("layer")
    row = lax.axis_index("row")
    x, z = row // ZS, row % ZS

    mats = (trans_hbm, refl_hbm, recv_hbm, mid_hbm)
    outs = (trans_out_hbm, bounced_hbm, heard_hbm, middle_hbm)

    def trace_copy(c):
        return pltpu.make_async_copy(
            traces_hbm.at[:, pl.ds(c * WIDE, WIDE)], g.at[c, x, z], tr_sem.at[c]
        )

    def mat_copy(j):
        return pltpu.make_async_copy(mats[j], a_v.at[j], in_sem.at[j])

    source_copy = pltpu.make_async_copy(sources_hbm, src_v, src_sem)

    for c in range(STREAMS):
        trace_copy(c).start()
    for j in range(4):
        mat_copy(j).start()
    source_copy.start()

    xs = {k: lax.rem(x + (k + XS), XS) for k in range(-2, 3)}
    zs = {k: lax.rem(z + (k + ZS), ZS) for k in range(-4, 5)}
    x_devices = {k: xs[k] * ZS + z for k in range(-2, 3)}
    z_devices = {k: x * ZS + zs[k] for k in range(-4, 5)}

    reach_x, reach_z = set(), set()
    for u in range(UNITS):
        for part, phase, _, back, to in COPIES[u]:
            if (part < 2) == (phase == 0):
                reach_x |= {(to - back) % XS, (back - to) % XS}
            else:
                reach_z |= {(to - back) % ZS, (back - to) % ZS}
    around = [xs[k if k <= 2 else k - XS] * ZS + z for k in sorted(reach_x)]
    around += [x * ZS + zs[k if k <= 4 else k - ZS] for k in sorted(reach_z)]

    barrier = pltpu.get_barrier_semaphore()
    for other in around:
        pl.semaphore_signal(barrier, inc=1, device_id=(layer, other), device_id_type=MESH)

    @pl.when(layer < LAYERS - 1)
    def _():
        pl.semaphore_signal(barrier, inc=1, device_id=(layer + 1, row), device_id_type=MESH)

    @pl.when(layer > 0)
    def _():
        pl.semaphore_signal(barrier, inc=1, device_id=(layer - 1, row), device_id_type=MESH)

    ends = jnp.where(layer > 0, 1, 0) + jnp.where(layer < LAYERS - 1, 1, 0)
    pl.semaphore_wait(barrier, len(around) + ends)

    def regions(u, copy, distance):
        part, phase, group, _, _ = copy
        start, size, way = split_of(u)[part]
        rows = pl.ds(start, size)
        along_x = (part < 2) == (phase == 0)
        if along_x:
            here = xs[-way * distance]
            if phase == 0:
                return [g.at[u, here, z, rows]]
            if len(Z_GROUPS[group]) == ZS:
                return [g.at[u, here, :, rows]]
            return [g.at[u, here, zs[-way * away], rows] for away in Z_GROUPS[group]]
        here = zs[-way * distance]
        if phase == 0:
            return [g.at[u, x, here, rows]]
        if len(X_GROUPS[group]) == XS:
            return [g.at[u, :, here, rows]]
        return [g.at[u, xs[-way * away], here, rows] for away in X_GROUPS[group]]

    def send(u, number):
        copy = COPIES[u][number]
        part, phase, _, back, to = copy
        way = split_of(u)[part][2]
        along_x = (part < 2) == (phase == 0)
        target = (x_devices if along_x else z_devices)[way * (to - back)]
        for moved in regions(u, copy, back):
            pltpu.make_async_remote_copy(
                src_ref=moved,
                dst_ref=moved,
                send_sem=send_sem.at[u],
                recv_sem=recv_sem.at[u, number],
                device_id=(layer, target),
                device_id_type=MESH,
            ).start()

    def receive(u, number):
        copy = COPIES[u][number]
        part, phase, group, _, to = copy
        moved = regions(u, copy, to)
        if len(moved) == 1:
            whole = moved[0]
        else:
            start, size, _ = split_of(u)[part]
            rows = pl.ds(start, size)
            whole = g.at[u, pl.ds(0, len(moved)), 0, rows] if part < 2 else g.at[u, 0, pl.ds(0, len(moved)), rows]
        pltpu.make_async_copy(whole, whole, recv_sem.at[u, number]).wait()

    def all_sent(u):
        whole = g.at[u].reshape(XS * ZS, ROWS, WIDE).at[pl.ds(0, XS * ZS - 1)]
        pltpu.make_async_copy(whole, whole, send_sem.at[u]).wait()

    def down(u):
        return pltpu.make_async_remote_copy(
            src_ref=sent_v.at[u],
            dst_ref=g.at[u + STREAMS, x, z],
            send_sem=pd_send.at[u],
            recv_sem=pd_recv.at[u],
            device_id=(lax.rem(layer + 1, LAYERS), row),
            device_id_type=MESH,
        )

    def dot(j, u):
        data = g[u].reshape(M, WIDE)
        return jnp.dot(a_v[j], data, preferred_element_type=jnp.float32)

    out_copies = []

    def put(j, t, c):
        columns = pl.ds(c * WIDE, WIDE)
        if j == 0:
            src, dst = out_v.at[0, :, columns], outs[0].at[:, columns]
        else:
            place = 1 + (j - 1) * TICKS + t
            src, dst = out_v.at[place, :, columns], outs[j].at[t, :, columns]
        copy = pltpu.make_async_copy(src, dst, out_sem.at[len(out_copies)])
        copy.start()
        out_copies.append(copy)

    waited = set()

    def need(j):
        if j not in waited:
            waited.add(j)
            if j == "sources":
                source_copy.wait()
            else:
                mat_copy(j).wait()

    here = {u: set() for u in range(UNITS)}
    gone = {u: set() for u in range(UNITS)}

    def send_ready(u):
        ready = [
            n
            for n, copy in enumerate(COPIES[u])
            if n not in gone[u] and all(needed in here[u] for needed in needs_of(copy))
        ]
        for n in sorted(ready, key=lambda n: send_key(u, COPIES[u][n])):
            gone[u].add(n)
            send(u, n)

    def begin(t, c, u):
        if t == 0:
            trace_copy(c).wait()
        else:

            @pl.when(layer > 0)
            def _():
                down(u - STREAMS).wait_recv()

            @pl.when(layer == 0)
            def _():
                g[u, x, z] = jnp.zeros((ROWS, WIDE), jnp.bfloat16)

        send_ready(u)

    def transmit(t, c, u):
        need(0)
        need("sources")
        columns = pl.ds(c * WIDE, WIDE)
        sent = dot(0, u) + src_v[t, :, columns].astype(jnp.float32)
        sent = sent.astype(jnp.bfloat16)
        if t + 1 < TICKS:
            sent_v[u] = sent

            @pl.when(layer < LAYERS - 1)
            def _():
                down(u).start()
        else:
            out_v[0, :, columns] = sent
            put(0, t, c)

    for task in ORDER:
        u, n = divmod(task, 100)
        t, c = divmod(u, STREAMS)
        if n == 90:
            begin(t, c, u)
        elif n == 91:
            transmit(t, c, u)
        elif n > 91:
            j = n - 91
            need(j)
            place = 1 + (j - 1) * TICKS + t
            out_v[place, :, pl.ds(c * WIDE, WIDE)] = dot(j, u).astype(jnp.bfloat16)
            put(j, t, c)
        else:
            receive(u, n)
            part, phase, group, _, to = COPIES[u][n]
            here[u].add((part, phase, group, to))
            send_ready(u)

    for u in range(UNITS):
        all_sent(u)

    @pl.when(layer < LAYERS - 1)
    def _():
        for u in range(UNITS - STREAMS):
            down(u).wait_send()

    for copy in out_copies:
        copy.wait()


def hand_on(*refs):
    n = (len(refs) - 2) // 3
    into, out, held = refs[:n], refs[n : 2 * n], refs[2 * n : 3 * n]
    in_sem, out_sem = refs[-2:]
    ins = [pltpu.make_async_copy(into[i], held[i], in_sem.at[i]) for i in range(n)]
    outs = [pltpu.make_async_copy(held[i], out[i], out_sem.at[i]) for i in range(n)]
    for copy in ins:
        copy.start()
    for i in range(n):
        ins[i].wait()
        outs[i].start()
    for copy in outs:
        copy.wait()


def shards(transmission, reflection, receiver_map, midplane_map, traces, sources):
    stacked = jax.ShapeDtypeStruct((TICKS, ROWS, B), jnp.bfloat16)
    n_outs = (TICKS * 3 + 1) * STREAMS
    results = pl.pallas_call(
        kernel,
        out_shape=(stacked, stacked, stacked, jax.ShapeDtypeStruct((ROWS, B), jnp.bfloat16)),
        in_specs=[pl.BlockSpec(memory_space=pl.ANY)] * 6,
        out_specs=[pl.BlockSpec(memory_space=pl.ANY)] * 4,
        scratch_shapes=[
            pltpu.VMEM((4, ROWS, M), jnp.bfloat16),
            pltpu.VMEM((UNITS, XS, ZS, ROWS, WIDE), jnp.bfloat16),
            pltpu.VMEM((TICKS, ROWS, B), jnp.bfloat16),
            pltpu.VMEM((UNITS - STREAMS, ROWS, WIDE), jnp.bfloat16),
            pltpu.VMEM((1 + 3 * TICKS, ROWS, B), jnp.bfloat16),
            pltpu.SemaphoreType.DMA((UNITS,)),
            pltpu.SemaphoreType.DMA((UNITS, len(COPIES[0]))),
            pltpu.SemaphoreType.DMA((UNITS - STREAMS,)),
            pltpu.SemaphoreType.DMA((UNITS - STREAMS,)),
            pltpu.SemaphoreType.DMA((4,)),
            pltpu.SemaphoreType.DMA((STREAMS,)),
            pltpu.SemaphoreType.DMA,
            pltpu.SemaphoreType.DMA((n_outs,)),
        ],
        compiler_params=pltpu.CompilerParams(
            collective_id=0, has_side_effects=True, vmem_limit_bytes=VMEM
        ),
    )(transmission[0], reflection[0], receiver_map[0], midplane_map[0], traces[0], sources[0])
    bounced, heard, middle, sent = pl.pallas_call(
        hand_on,
        out_shape=tuple(jax.ShapeDtypeStruct(r.shape, r.dtype) for r in results),
        in_specs=[pl.BlockSpec(memory_space=pl.ANY)] * 4,
        out_specs=[pl.BlockSpec(memory_space=pl.ANY)] * 4,
        scratch_shapes=[pltpu.VMEM(r.shape, r.dtype) for r in results]
        + [pltpu.SemaphoreType.DMA((4,)), pltpu.SemaphoreType.DMA((4,))],
        compiler_params=pltpu.CompilerParams(vmem_limit_bytes=VMEM),
    )(*results)
    return bounced[None], heard[None], middle[None], sent[None]


def solution(mesh):
    return jax.shard_map(
        shards,
        mesh=mesh,
        in_specs=(
            P("layer", "row", None),
            P("layer", "row", None),
            P("layer", "row", None),
            P("layer", "row", None),
            P("layer", "row", None),
            P("layer", None, "row", None),
        ),
        out_specs=(
            P("layer", None, "row", None),
            P("layer", None, "row", None),
            P("layer", None, "row", None),
            P("layer", "row", None),
        ),
        check_vma=False,
    )
```

```python
import functools

import jax
import jax.numpy as jnp
from jax import lax
from jax.experimental import pallas as pl
from jax.experimental.pallas import tpu as pltpu
from jax.sharding import PartitionSpec as P

MESH = pl.DeviceIdType.MESH

TICKS = 3
LAYERS = 8
XS, ZS = 4, 8
ROWS = 192
M = XS * ZS * ROWS
B = 384
WIDE = 128
STREAMS = B // WIDE
VMEM = 62 * 1024 * 1024
UNITS = TICKS * STREAMS

SPLITS = (
    ((0, 32, 1), (32, 32, -1), (64, 64, 1), (128, 64, -1)),
    ((0, 48, 1), (48, 48, -1), (96, 48, 1), (144, 48, -1)),
    ((0, 32, 1), (32, 16, -1), (48, 80, 1), (128, 64, -1)),
    ((0, 16, 1), (16, 16, -1), (32, 80, 1), (112, 80, -1)),
)
X_TREES = (
    ((0, 1), (0, -1), (1, 2)),
    ((0, 1), (0, -1), (0, 2)),
)
Z_TREES = (
    ((0, 1), (0, -1), (1, 2), (-1, -2), (2, 3), (-2, -3), (3, 4)),
    ((0, 1), (0, -1), (0, 2), (0, -2), (2, 3), (-2, -3), (3, 4)),
    ((0, 1), (0, -1), (0, 2), (0, -2), (2, 3), (-2, -3), (2, 4)),
    ((0, 1), (0, -1), (0, 2), (0, -2), (0, 3), (0, -3), (0, 4)),
)
PLANS = (
    (0, 1, 0, 2, 0),
    (3, 0, 0, 0, 0),
    (1, 1, 0, 1, 0),
    (2, 1, 0, 2, 0),
    (0, 1, 0, 1, 0),
    (1, 1, 0, 1, 0),
    (3, 1, 1, 2, 0),
    (1, 1, 0, 2, 0),
    (1, 1, 0, 2, 0),
)
X_GROUPS = ((0, 1, -1, 2),)
Z_GROUPS = ((0, 1, -1), (2, -2, 3, -3, 4))

ORDER = (
    90, 190, 290, 0, 1, 11, 10, 100, 101, 12, 110, 111, 2, 22, 23, 20, 21, 36, 35, 34, 33, 120, 121, 134, 133, 211,
    210, 112, 212, 102, 222, 223, 234, 233, 236, 235, 220, 14, 13, 221, 27, 28, 3, 4, 200, 25, 201, 202, 41, 40, 24,
    26, 38, 37, 39, 136, 135, 114, 113, 127, 122, 123, 128, 141, 140, 214, 213, 103, 104, 241, 224, 240, 238, 237,
    225, 227, 16, 15, 228, 5, 6, 29, 42, 203, 204, 138, 137, 116, 30, 31, 115, 124, 125, 216, 215, 44, 105, 43, 106,
    239, 18, 17, 226, 7, 8, 142, 129, 229, 242, 205, 206, 118, 139, 117, 32, 126, 218, 217, 45, 107, 108, 244, 9, 19,
    91, 119, 243, 230, 207, 208, 231, 109, 92, 144, 219, 93, 390, 143, 94, 130, 335, 336, 333, 334, 311, 323, 322,
    321, 320, 310, 300, 302, 301, 131, 312, 232, 209, 245, 291, 338, 337, 339, 325, 145, 132, 191, 340, 341, 313, 314,
    324, 304, 326, 303, 328, 327, 590, 523, 522, 521, 520, 533, 535, 510, 512, 534, 511, 536, 490, 501, 500, 502, 343,
    344, 422, 423, 292, 316, 315, 410, 411, 412, 305, 342, 306, 436, 435, 434, 433, 537, 420, 421, 330, 514, 538, 513,
    524, 525, 401, 400, 331, 402, 293, 329, 425, 424, 528, 504, 317, 318, 503, 527, 540, 413, 414, 541, 294, 308, 307,
    437, 441, 438, 539, 345, 192, 440, 516, 515, 427, 404, 403, 526, 428, 426, 319, 332, 542, 506, 505, 193, 415, 416,
    439, 309, 391, 442, 543, 544, 517, 518, 529, 429, 406, 405, 531, 508, 507, 530, 417, 194, 418, 431, 392, 430, 690,
    393, 443, 622, 623, 601, 444, 610, 620, 621, 612, 636, 407, 545, 635, 611, 519, 634, 633, 532, 509, 591, 419, 408,
    625, 600, 432, 602, 624, 626, 445, 638, 394, 409, 491, 890, 637, 639, 641, 614, 613, 616, 615, 640, 811, 822, 820,
    823, 834, 836, 810, 812, 833, 835, 821, 790, 800, 802, 801, 627, 628, 603, 604, 605, 606, 630, 722, 723, 720, 734,
    733, 711, 736, 735, 710, 712, 721, 700, 702, 701, 838, 813, 825, 824, 826, 814, 837, 841, 839, 803, 804, 827, 618,
    617, 644, 643, 725, 724, 642, 631, 738, 726, 737, 739, 714, 840, 713, 828, 740, 607, 608, 629, 703, 592, 728, 704,
    632, 816, 741, 815, 593, 727, 831, 805, 806, 594, 843, 716, 830, 715, 619, 609, 492, 705, 844, 706, 493, 829, 818,
    645, 691, 817, 731, 807, 730, 808, 494, 718, 743, 744, 717, 692, 729, 707, 842, 708, 693, 742, 694, 819, 832, 809,
    845, 891, 732, 892, 719, 745, 893, 709, 791, 894, 792, 793, 794,
)

def copies_of(u):
    found = []
    _, x_first, z_second, z_first, x_second = PLANS[u]
    for part in range(4):
        first, second, groups = (
            (X_TREES[x_first], Z_TREES[z_second], X_GROUPS) if part < 2 else (Z_TREES[z_first], X_TREES[x_second], Z_GROUPS)
        )
        for back, to in first:
            found.append((part, 0, None, back, to))
        for group in range(len(groups)):
            for back, to in second:
                found.append((part, 1, group, back, to))
    return found


OWN = "own traces"


def needs_of(copy):
    part, phase, group, back, _ = copy
    if phase == 0:
        return [] if back == 0 else [(part, 0, None, back)]
    if back != 0:
        return [(part, 1, group, back)]
    groups = X_GROUPS if part < 2 else Z_GROUPS
    return [(part, 0, None, away) if away else OWN for away in groups[group]]


COPIES = [copies_of(u) for u in range(UNITS)]


def split_of(u):
    return SPLITS[PLANS[u][0]]


def size_of(u, copy):
    part, phase, group, _, _ = copy
    groups = X_GROUPS if part < 2 else Z_GROUPS
    return split_of(u)[part][1] * (len(groups[group]) if phase else 1)


def send_key(u, copy):
    rows, phase, far = size_of(u, copy), copy[1], abs(copy[4] - copy[3])
    return (phase, -far, rows)


def kernel(
    trans_hbm, refl_hbm, recv_hbm, mid_hbm, traces_hbm, sources_hbm,
    bounced_hbm, heard_hbm, middle_hbm, trans_out_hbm,
    a_v, g, src_v, sent_v, out_v,
    send_sem, recv_sem, pd_send, pd_recv, in_sem, tr_sem, src_sem, out_sem,
):
    layer = lax.axis_index("layer")
    row = lax.axis_index("row")
    x, z = row // ZS, row % ZS
    behind, before = lax.rem(layer + 1, LAYERS), lax.rem(layer + LAYERS - 1, LAYERS)

    mats = (trans_hbm, refl_hbm, recv_hbm, mid_hbm)
    outs = (trans_out_hbm, bounced_hbm, heard_hbm, middle_hbm)

    def trace_copy(c):
        return pltpu.make_async_copy(
            traces_hbm.at[:, pl.ds(c * WIDE, WIDE)], g.at[c, x, z], tr_sem.at[c]
        )

    def mat_copy(j):
        return pltpu.make_async_copy(mats[j], a_v.at[j], in_sem.at[j])

    source_copy = pltpu.make_async_copy(sources_hbm, src_v, src_sem)

    for c in range(STREAMS):
        trace_copy(c).start()
    for j in range(4):
        mat_copy(j).start()
    source_copy.start()

    xs = {k: lax.rem(x + (k + XS), XS) for k in range(-2, 3)}
    zs = {k: lax.rem(z + (k + ZS), ZS) for k in range(-4, 5)}
    x_devices = {k: xs[k] * ZS + z for k in range(-2, 3)}
    z_devices = {k: x * ZS + zs[k] for k in range(-4, 5)}

    own, following = set(), {(0, 0)}
    for u in range(UNITS):
        for part, phase, _, back, to in COPIES[u]:
            from_behind = u >= STREAMS and phase == 0 and back == 0
            for step in (to - back, back - to):
                if (part < 2) == (phase == 0):
                    place = ((step + XS // 2 - 1) % XS - (XS // 2 - 1), 0)
                else:
                    place = (0, (step + ZS // 2 - 1) % ZS - (ZS // 2 - 1))
                (following if from_behind else own).add(place)

    barrier = pltpu.get_barrier_semaphore()
    for section, places in ((layer, own), (before, following)):
        for dx, dz in sorted(places):
            pl.semaphore_signal(barrier, inc=1, device_id=(section, xs[dx] * ZS + zs[dz]), device_id_type=MESH)
    pl.semaphore_wait(barrier, len(own) + len(following))

    def regions(u, copy, distance):
        part, phase, group, _, _ = copy
        start, size, way = split_of(u)[part]
        rows = pl.ds(start, size)
        along_x = (part < 2) == (phase == 0)
        if along_x:
            here = xs[-way * distance]
            if phase == 0:
                return [g.at[u, here, z, rows]]
            if len(Z_GROUPS[group]) == ZS:
                return [g.at[u, here, :, rows]]
            return [g.at[u, here, zs[-way * away], rows] for away in Z_GROUPS[group]]
        here = zs[-way * distance]
        if phase == 0:
            return [g.at[u, x, here, rows]]
        if len(X_GROUPS[group]) == XS:
            return [g.at[u, :, here, rows]]
        return [g.at[u, xs[-way * away], here, rows] for away in X_GROUPS[group]]

    def send(u, number):
        copy = COPIES[u][number]
        part, phase, _, back, to = copy
        way = split_of(u)[part][2]
        along_x = (part < 2) == (phase == 0)
        target = (x_devices if along_x else z_devices)[way * (to - back)]
        if phase == 0 and back == 0 and u >= STREAMS:
            start, size, _ = split_of(u)[part]
            pltpu.make_async_remote_copy(
                src_ref=sent_v.at[u - STREAMS, pl.ds(start, size)],
                dst_ref=g.at[u, x, z, pl.ds(start, size)],
                send_sem=send_sem.at[u],
                recv_sem=recv_sem.at[u, number],
                device_id=(behind, target),
                device_id_type=MESH,
            ).start()
            return
        for moved in regions(u, copy, back):
            pltpu.make_async_remote_copy(
                src_ref=moved,
                dst_ref=moved,
                send_sem=send_sem.at[u],
                recv_sem=recv_sem.at[u, number],
                device_id=(layer, target),
                device_id_type=MESH,
            ).start()

    def receive(u, number):
        copy = COPIES[u][number]
        part, phase, group, _, to = copy
        moved = regions(u, copy, to)
        if len(moved) == 1:
            whole = moved[0]
        else:
            start, size, _ = split_of(u)[part]
            rows = pl.ds(start, size)
            whole = g.at[u, pl.ds(0, len(moved)), 0, rows] if part < 2 else g.at[u, 0, pl.ds(0, len(moved)), rows]
        pltpu.make_async_copy(whole, whole, recv_sem.at[u, number]).wait()

    def all_sent(u):
        whole = g.at[u].reshape(XS * ZS, ROWS, WIDE).at[pl.ds(0, XS * ZS - 1)]
        pltpu.make_async_copy(whole, whole, send_sem.at[u]).wait()

    def down(u):
        return pltpu.make_async_remote_copy(
            src_ref=sent_v.at[u],
            dst_ref=g.at[u + STREAMS, x, z],
            send_sem=pd_send.at[u],
            recv_sem=pd_recv.at[u],
            device_id=(behind, row),
            device_id_type=MESH,
        )

    def dot(j, u):
        data = g[u].reshape(M, WIDE)
        return jnp.dot(a_v[j], data, preferred_element_type=jnp.float32)

    out_copies = []

    def put(j, t, c):
        columns = pl.ds(c * WIDE, WIDE)
        if j == 0:
            src, dst = out_v.at[0, :, columns], outs[0].at[:, columns]
        else:
            place = 1 + (j - 1) * TICKS + t
            src, dst = out_v.at[place, :, columns], outs[j].at[t, :, columns]
        copy = pltpu.make_async_copy(src, dst, out_sem.at[len(out_copies)])
        copy.start()
        out_copies.append(copy)

    waited = set()

    def need(j):
        if j not in waited:
            waited.add(j)
            if j == "sources":
                source_copy.wait()
            else:
                mat_copy(j).wait()

    here = {u: set() for u in range(UNITS)}
    gone = {u: set() for u in range(UNITS)}

    def send_ready(u, phases=(0, 1)):
        ready = [
            n
            for n, copy in enumerate(COPIES[u])
            if n not in gone[u] and copy[1] in phases and all(needed in here[u] for needed in needs_of(copy))
        ]
        for n in sorted(ready, key=lambda n: send_key(u, COPIES[u][n])):
            gone[u].add(n)
            send(u, n)

    def begin(t, c, u):
        if t == 0:
            trace_copy(c).wait()
        else:
            down(u - STREAMS).wait_recv()
        here[u].add(OWN)
        send_ready(u)

    def kept(t, value):
        return value if t == 0 else jnp.where(layer == 0, 0.0, value)

    def transmit(t, c, u):
        need(0)
        need("sources")
        columns = pl.ds(c * WIDE, WIDE)
        sent = kept(t, dot(0, u)) + src_v[t, :, columns].astype(jnp.float32)
        sent = sent.astype(jnp.bfloat16)
        if t + 1 < TICKS:
            sent_v[u] = sent
            down(u).start()
            send_ready(u + STREAMS, (0,))
        else:
            out_v[0, :, columns] = sent
            put(0, t, c)

    for task in ORDER:
        u, n = divmod(task, 100)
        t, c = divmod(u, STREAMS)
        if n == 90:
            begin(t, c, u)
        elif n == 91:
            transmit(t, c, u)
        elif n > 91:
            j = n - 91
            need(j)
            place = 1 + (j - 1) * TICKS + t
            out_v[place, :, pl.ds(c * WIDE, WIDE)] = kept(t, dot(j, u)).astype(jnp.bfloat16)
            put(j, t, c)
        else:
            receive(u, n)
            part, phase, group, _, to = COPIES[u][n]
            here[u].add((part, phase, group, to))
            send_ready(u)

    for u in range(UNITS):
        all_sent(u)

    for u in range(UNITS - STREAMS):
        down(u).wait_send()

    for copy in out_copies:
        copy.wait()


def hand_on(*refs):
    n = (len(refs) - 2) // 3
    into, out, held = refs[:n], refs[n : 2 * n], refs[2 * n : 3 * n]
    in_sem, out_sem = refs[-2:]
    ins = [pltpu.make_async_copy(into[i], held[i], in_sem.at[i]) for i in range(n)]
    outs = [pltpu.make_async_copy(held[i], out[i], out_sem.at[i]) for i in range(n)]
    for copy in ins:
        copy.start()
    for i in range(n):
        ins[i].wait()
        outs[i].start()
    for copy in outs:
        copy.wait()


def shards(transmission, reflection, receiver_map, midplane_map, traces, sources):
    stacked = jax.ShapeDtypeStruct((TICKS, ROWS, B), jnp.bfloat16)
    n_outs = (TICKS * 3 + 1) * STREAMS
    results = pl.pallas_call(
        kernel,
        out_shape=(stacked, stacked, stacked, jax.ShapeDtypeStruct((ROWS, B), jnp.bfloat16)),
        in_specs=[pl.BlockSpec(memory_space=pl.ANY)] * 6,
        out_specs=[pl.BlockSpec(memory_space=pl.ANY)] * 4,
        scratch_shapes=[
            pltpu.VMEM((4, ROWS, M), jnp.bfloat16),
            pltpu.VMEM((UNITS, XS, ZS, ROWS, WIDE), jnp.bfloat16),
            pltpu.VMEM((TICKS, ROWS, B), jnp.bfloat16),
            pltpu.VMEM((UNITS - STREAMS, ROWS, WIDE), jnp.bfloat16),
            pltpu.VMEM((1 + 3 * TICKS, ROWS, B), jnp.bfloat16),
            pltpu.SemaphoreType.DMA((UNITS,)),
            pltpu.SemaphoreType.DMA((UNITS, len(COPIES[0]))),
            pltpu.SemaphoreType.DMA((UNITS - STREAMS,)),
            pltpu.SemaphoreType.DMA((UNITS - STREAMS,)),
            pltpu.SemaphoreType.DMA((4,)),
            pltpu.SemaphoreType.DMA((STREAMS,)),
            pltpu.SemaphoreType.DMA,
            pltpu.SemaphoreType.DMA((n_outs,)),
        ],
        compiler_params=pltpu.CompilerParams(
            collective_id=0, has_side_effects=True, vmem_limit_bytes=VMEM
        ),
    )(transmission[0], reflection[0], receiver_map[0], midplane_map[0], traces[0], sources[0])
    bounced, heard, middle, sent = pl.pallas_call(
        hand_on,
        out_shape=tuple(jax.ShapeDtypeStruct(r.shape, r.dtype) for r in results),
        in_specs=[pl.BlockSpec(memory_space=pl.ANY)] * 4,
        out_specs=[pl.BlockSpec(memory_space=pl.ANY)] * 4,
        scratch_shapes=[pltpu.VMEM(r.shape, r.dtype) for r in results]
        + [pltpu.SemaphoreType.DMA((4,)), pltpu.SemaphoreType.DMA((4,))],
        compiler_params=pltpu.CompilerParams(vmem_limit_bytes=VMEM),
    )(*results)
    return bounced[None], heard[None], middle[None], sent[None]


def solution(mesh):
    return jax.shard_map(
        shards,
        mesh=mesh,
        in_specs=(
            P("layer", "row", None),
            P("layer", "row", None),
            P("layer", "row", None),
            P("layer", "row", None),
            P("layer", "row", None),
            P("layer", None, "row", None),
        ),
        out_specs=(
            P("layer", None, "row", None),
            P("layer", None, "row", None),
            P("layer", None, "row", None),
            P("layer", "row", None),
        ),
        check_vma=False,
    )
```

```python
import functools

import jax
import jax.numpy as jnp
from jax import lax
from jax.experimental import pallas as pl
from jax.experimental.pallas import tpu as pltpu
from jax.sharding import PartitionSpec as P

MESH = pl.DeviceIdType.MESH

TICKS = 3
LAYERS = 8
XS, ZS = 4, 8
ROWS = 192
M = XS * ZS * ROWS
B = 384
WIDE = 128
STREAMS = B // WIDE
VMEM = 62 * 1024 * 1024
UNITS = TICKS * STREAMS

SPLITS = (
    ((0, 32, 1), (32, 32, -1), (64, 64, 1), (128, 64, -1)),
    ((0, 32, 1), (32, 48, -1), (80, 64, 1), (144, 48, -1)),
    ((0, 48, 1), (48, 32, -1), (80, 48, 1), (128, 64, -1)),
    ((0, 48, 1), (48, 48, -1), (96, 48, 1), (144, 48, -1)),
    ((0, 32, 1), (32, 32, -1), (64, 64, -1), (128, 64, 1)),
    ((0, 16, 1), (16, 32, -1), (48, 64, 1), (112, 80, -1)),
)
X_TREES = (
    ((0, 1), (0, -1), (1, 2)),
    ((0, 1), (0, -1), (0, 2)),
)
Z_TREES = (
    ((0, 1), (0, -1), (1, 2), (-1, -2), (2, 3), (-2, -3), (3, 4)),
    ((0, 1), (0, -1), (0, 2), (0, -2), (2, 3), (-2, -3), (3, 4)),
    ((0, 1), (0, -1), (0, 2), (0, -2), (2, 3), (-2, -3), (2, 4)),
    ((0, 1), (0, -1), (0, 2), (0, -2), (0, 3), (0, -3), (0, 4)),
)
PLANS = (
    (2, 1, 0, 2, 0),
    (0, 0, 0, 2, 0),
    (4, 0, 0, 0, 0),
    (4, 1, 1, 2, 0),
    (4, 0, 0, 2, 0),
    (3, 1, 0, 1, 0),
    (5, 1, 0, 2, 0),
    (3, 1, 0, 2, 0),
    (1, 1, 0, 2, 0),
)
X_GROUPS = ((0, 1, -1, 2),)
Z_GROUPS = ((0, 1, -1), (2, -2, 3, -3, 4))

ORDER = (
    90, 190, 10, 11, 0, 20, 21, 1, 12, 290, 22, 23, 2, 34, 100, 101, 111, 110, 120, 121, 33, 36, 35, 134, 133, 122,
    123, 27, 200, 211, 201, 210, 28, 136, 135, 14, 102, 221, 220, 233, 234, 24, 25, 112, 127, 128, 13, 4, 26, 3, 37,
    41, 38, 40, 124, 125, 141, 39, 212, 137, 138, 126, 202, 227, 104, 139, 222, 223, 236, 228, 235, 103, 241, 140,
    240, 29, 16, 113, 114, 31, 15, 129, 5, 6, 42, 214, 213, 30, 203, 204, 225, 43, 237, 106, 224, 44, 105, 238, 18,
    115, 131, 116, 17, 130, 229, 7, 8, 216, 215, 144, 143, 205, 206, 239, 242, 108, 107, 142, 226, 118, 32, 117, 19,
    45, 9, 91, 208, 207, 217, 218, 132, 92, 109, 145, 93, 243, 119, 191, 320, 321, 390, 300, 244, 231, 230, 311, 334,
    333, 322, 323, 310, 302, 301, 209, 219, 94, 312, 401, 336, 410, 420, 421, 245, 335, 490, 400, 411, 327, 434, 433,
    422, 324, 325, 423, 328, 192, 303, 232, 291, 326, 304, 305, 412, 402, 306, 340, 341, 314, 313, 436, 435, 428, 427,
    329, 440, 337, 193, 500, 338, 590, 316, 424, 425, 315, 441, 339, 511, 520, 510, 501, 502, 426, 521, 522, 512, 307,
    331, 330, 523, 342, 534, 533, 536, 535, 429, 404, 403, 442, 413, 437, 414, 194, 308, 438, 292, 344, 317, 343, 318,
    439, 504, 503, 524, 293, 430, 525, 528, 431, 537, 513, 527, 514, 309, 294, 406, 538, 541, 415, 405, 332, 319, 416,
    540, 345, 391, 526, 506, 505, 539, 408, 407, 529, 444, 443, 432, 515, 516, 417, 418, 392, 542, 600, 690, 611, 393,
    620, 621, 610, 601, 602, 530, 531, 622, 623, 612, 634, 633, 544, 394, 507, 508, 543, 409, 636, 517, 635, 445, 518,
    419, 491, 624, 625, 603, 604, 628, 627, 626, 532, 640, 613, 614, 492, 509, 545, 519, 591, 720, 710, 711, 700, 721,
    701, 702, 790, 722, 712, 734, 605, 733, 723, 606, 736, 638, 637, 639, 890, 735, 641, 629, 631, 630, 800, 833, 834,
    811, 642, 616, 801, 802, 821, 820, 810, 835, 836, 727, 728, 741, 704, 823, 822, 812, 724, 703, 740, 615, 713, 493,
    725, 726, 608, 737, 607, 738, 714, 644, 643, 739, 804, 837, 840, 803, 632, 838, 618, 494, 824, 839, 825, 706, 828,
    841, 742, 826, 827, 814, 813, 731, 729, 592, 705, 617, 609, 593, 730, 715, 716, 806, 645, 594, 805, 744, 708, 743,
    816, 844, 842, 815, 707, 619, 691, 843, 830, 718, 717, 692, 807, 808, 829, 831, 693, 818, 732, 817, 694, 709, 745,
    845, 719, 791, 809, 832, 792, 793, 819, 891, 794, 892, 893, 894,
)

def copies_of(u):
    found = []
    _, x_first, z_second, z_first, x_second = PLANS[u]
    for part in range(4):
        first, second, groups = (
            (X_TREES[x_first], Z_TREES[z_second], X_GROUPS) if part < 2 else (Z_TREES[z_first], X_TREES[x_second], Z_GROUPS)
        )
        for back, to in first:
            found.append((part, 0, None, back, to))
        for group in range(len(groups)):
            for back, to in second:
                found.append((part, 1, group, back, to))
    return found


OWN = "own traces"


def needs_of(copy):
    part, phase, group, back, _ = copy
    if phase == 0:
        return [] if back == 0 else [(part, 0, None, back)]
    if back != 0:
        return [(part, 1, group, back)]
    groups = X_GROUPS if part < 2 else Z_GROUPS
    return [(part, 0, None, away) if away else OWN for away in groups[group]]


COPIES = [copies_of(u) for u in range(UNITS)]


def split_of(u):
    return SPLITS[PLANS[u][0]]


def size_of(u, copy):
    part, phase, group, _, _ = copy
    groups = X_GROUPS if part < 2 else Z_GROUPS
    return split_of(u)[part][1] * (len(groups[group]) if phase else 1)


def send_key(u, copy):
    rows, phase, far = size_of(u, copy), copy[1], abs(copy[4] - copy[3])
    return (-phase, rows)


def kernel(
    trans_hbm, refl_hbm, recv_hbm, mid_hbm, traces_hbm, sources_hbm,
    bounced_hbm, heard_hbm, middle_hbm, trans_out_hbm,
    a_v, g, src_v, sent_v, out_v,
    send_sem, recv_sem, pd_send, pd_recv, in_sem, tr_sem, src_sem, out_sem,
):
    layer = lax.axis_index("layer")
    row = lax.axis_index("row")
    x, z = row // ZS, row % ZS
    behind, before = lax.rem(layer + 1, LAYERS), lax.rem(layer + LAYERS - 1, LAYERS)

    mats = (trans_hbm, refl_hbm, recv_hbm, mid_hbm)
    outs = (trans_out_hbm, bounced_hbm, heard_hbm, middle_hbm)

    def trace_copy(c):
        return pltpu.make_async_copy(
            traces_hbm.at[:, pl.ds(c * WIDE, WIDE)], g.at[c, x, z], tr_sem.at[c]
        )

    def mat_copy(j):
        return pltpu.make_async_copy(mats[j], a_v.at[j], in_sem.at[j])

    source_copy = pltpu.make_async_copy(sources_hbm, src_v, src_sem)

    for c in range(STREAMS):
        trace_copy(c).start()
    for j in range(4):
        mat_copy(j).start()
    source_copy.start()

    xs = {k: lax.rem(x + (k + XS), XS) for k in range(-2, 3)}
    zs = {k: lax.rem(z + (k + ZS), ZS) for k in range(-4, 5)}
    x_devices = {k: xs[k] * ZS + z for k in range(-2, 3)}
    z_devices = {k: x * ZS + zs[k] for k in range(-4, 5)}

    own, following = set(), {(0, 0)}
    for u in range(UNITS):
        for part, phase, _, back, to in COPIES[u]:
            from_behind = u >= STREAMS and phase == 0 and back == 0
            for step in (to - back, back - to):
                if (part < 2) == (phase == 0):
                    place = ((step + XS // 2 - 1) % XS - (XS // 2 - 1), 0)
                else:
                    place = (0, (step + ZS // 2 - 1) % ZS - (ZS // 2 - 1))
                (following if from_behind else own).add(place)

    barrier = pltpu.get_barrier_semaphore()
    for section, places in ((layer, own), (before, following)):
        for dx, dz in sorted(places):
            pl.semaphore_signal(barrier, inc=1, device_id=(section, xs[dx] * ZS + zs[dz]), device_id_type=MESH)
    pl.semaphore_wait(barrier, len(own) + len(following))

    def regions(u, copy, distance):
        part, phase, group, _, _ = copy
        start, size, way = split_of(u)[part]
        rows = pl.ds(start, size)
        along_x = (part < 2) == (phase == 0)
        if along_x:
            here = xs[-way * distance]
            if phase == 0:
                return [g.at[u, here, z, rows]]
            if len(Z_GROUPS[group]) == ZS:
                return [g.at[u, here, :, rows]]
            return [g.at[u, here, zs[-way * away], rows] for away in Z_GROUPS[group]]
        here = zs[-way * distance]
        if phase == 0:
            return [g.at[u, x, here, rows]]
        if len(X_GROUPS[group]) == XS:
            return [g.at[u, :, here, rows]]
        return [g.at[u, xs[-way * away], here, rows] for away in X_GROUPS[group]]

    def send(u, number):
        copy = COPIES[u][number]
        part, phase, _, back, to = copy
        way = split_of(u)[part][2]
        along_x = (part < 2) == (phase == 0)
        target = (x_devices if along_x else z_devices)[way * (to - back)]
        if phase == 0 and back == 0 and u >= STREAMS:
            start, size, _ = split_of(u)[part]
            pltpu.make_async_remote_copy(
                src_ref=sent_v.at[u - STREAMS, pl.ds(start, size)],
                dst_ref=g.at[u, x, z, pl.ds(start, size)],
                send_sem=send_sem.at[u],
                recv_sem=recv_sem.at[u, number],
                device_id=(behind, target),
                device_id_type=MESH,
            ).start()
            return
        for moved in regions(u, copy, back):
            pltpu.make_async_remote_copy(
                src_ref=moved,
                dst_ref=moved,
                send_sem=send_sem.at[u],
                recv_sem=recv_sem.at[u, number],
                device_id=(layer, target),
                device_id_type=MESH,
            ).start()

    def receive(u, number):
        copy = COPIES[u][number]
        part, phase, group, _, to = copy
        moved = regions(u, copy, to)
        if len(moved) == 1:
            whole = moved[0]
        else:
            start, size, _ = split_of(u)[part]
            rows = pl.ds(start, size)
            whole = g.at[u, pl.ds(0, len(moved)), 0, rows] if part < 2 else g.at[u, 0, pl.ds(0, len(moved)), rows]
        pltpu.make_async_copy(whole, whole, recv_sem.at[u, number]).wait()

    def all_sent(u):
        whole = g.at[u].reshape(XS * ZS, ROWS, WIDE).at[pl.ds(0, XS * ZS - 1)]
        pltpu.make_async_copy(whole, whole, send_sem.at[u]).wait()

    def down(u):
        return pltpu.make_async_remote_copy(
            src_ref=sent_v.at[u],
            dst_ref=g.at[u + STREAMS, x, z],
            send_sem=pd_send.at[u],
            recv_sem=pd_recv.at[u],
            device_id=(behind, row),
            device_id_type=MESH,
        )

    def dot(j, u):
        data = g[u].reshape(M, WIDE)
        return jnp.dot(a_v[j], data, preferred_element_type=jnp.float32)

    out_copies = []

    def put(j, t, c):
        columns = pl.ds(c * WIDE, WIDE)
        if j == 0:
            src, dst = out_v.at[0, :, columns], outs[0].at[:, columns]
        else:
            place = 1 + (j - 1) * TICKS + t
            src, dst = out_v.at[place, :, columns], outs[j].at[t, :, columns]
        copy = pltpu.make_async_copy(src, dst, out_sem.at[len(out_copies)])
        copy.start()
        out_copies.append(copy)

    waited = set()

    def need(j):
        if j not in waited:
            waited.add(j)
            if j == "sources":
                source_copy.wait()
            else:
                mat_copy(j).wait()

    here = {u: set() for u in range(UNITS)}
    gone = {u: set() for u in range(UNITS)}

    def send_ready(u, phases=(0, 1)):
        ready = [
            n
            for n, copy in enumerate(COPIES[u])
            if n not in gone[u] and copy[1] in phases and all(needed in here[u] for needed in needs_of(copy))
        ]
        for n in sorted(ready, key=lambda n: send_key(u, COPIES[u][n])):
            gone[u].add(n)
            send(u, n)

    def begin(t, c, u):
        if t == 0:
            trace_copy(c).wait()
        else:
            down(u - STREAMS).wait_recv()
        here[u].add(OWN)
        send_ready(u)

    def kept(t, value):
        return value if t == 0 else jnp.where(layer == 0, 0.0, value)

    def transmit(t, c, u):
        need(0)
        need("sources")
        columns = pl.ds(c * WIDE, WIDE)
        sent = kept(t, dot(0, u)) + src_v[t, :, columns].astype(jnp.float32)
        sent = sent.astype(jnp.bfloat16)
        if t + 1 < TICKS:
            sent_v[u] = sent
            down(u).start()
            send_ready(u + STREAMS, (0,))
        else:
            out_v[0, :, columns] = sent
            put(0, t, c)

    for task in ORDER:
        u, n = divmod(task, 100)
        t, c = divmod(u, STREAMS)
        if n == 90:
            begin(t, c, u)
        elif n == 91:
            transmit(t, c, u)
        elif n > 91:
            j = n - 91
            need(j)
            place = 1 + (j - 1) * TICKS + t
            out_v[place, :, pl.ds(c * WIDE, WIDE)] = kept(t, dot(j, u)).astype(jnp.bfloat16)
            put(j, t, c)
        else:
            receive(u, n)
            part, phase, group, _, to = COPIES[u][n]
            here[u].add((part, phase, group, to))
            send_ready(u)

    for u in range(UNITS):
        all_sent(u)

    for u in range(UNITS - STREAMS):
        down(u).wait_send()

    for copy in out_copies:
        copy.wait()


def hand_on(*refs):
    n = (len(refs) - 2) // 3
    into, out, held = refs[:n], refs[n : 2 * n], refs[2 * n : 3 * n]
    in_sem, out_sem = refs[-2:]
    ins = [pltpu.make_async_copy(into[i], held[i], in_sem.at[i]) for i in range(n)]
    outs = [pltpu.make_async_copy(held[i], out[i], out_sem.at[i]) for i in range(n)]
    for copy in ins:
        copy.start()
    for i in range(n):
        ins[i].wait()
        outs[i].start()
    for copy in outs:
        copy.wait()


def shards(transmission, reflection, receiver_map, midplane_map, traces, sources):
    stacked = jax.ShapeDtypeStruct((TICKS, ROWS, B), jnp.bfloat16)
    n_outs = (TICKS * 3 + 1) * STREAMS
    results = pl.pallas_call(
        kernel,
        out_shape=(stacked, stacked, stacked, jax.ShapeDtypeStruct((ROWS, B), jnp.bfloat16)),
        in_specs=[pl.BlockSpec(memory_space=pl.ANY)] * 6,
        out_specs=[pl.BlockSpec(memory_space=pl.ANY)] * 4,
        scratch_shapes=[
            pltpu.VMEM((4, ROWS, M), jnp.bfloat16),
            pltpu.VMEM((UNITS, XS, ZS, ROWS, WIDE), jnp.bfloat16),
            pltpu.VMEM((TICKS, ROWS, B), jnp.bfloat16),
            pltpu.VMEM((UNITS - STREAMS, ROWS, WIDE), jnp.bfloat16),
            pltpu.VMEM((1 + 3 * TICKS, ROWS, B), jnp.bfloat16),
            pltpu.SemaphoreType.DMA((UNITS,)),
            pltpu.SemaphoreType.DMA((UNITS, len(COPIES[0]))),
            pltpu.SemaphoreType.DMA((UNITS - STREAMS,)),
            pltpu.SemaphoreType.DMA((UNITS - STREAMS,)),
            pltpu.SemaphoreType.DMA((4,)),
            pltpu.SemaphoreType.DMA((STREAMS,)),
            pltpu.SemaphoreType.DMA,
            pltpu.SemaphoreType.DMA((n_outs,)),
        ],
        compiler_params=pltpu.CompilerParams(
            collective_id=0, has_side_effects=True, vmem_limit_bytes=VMEM
        ),
    )(transmission[0], reflection[0], receiver_map[0], midplane_map[0], traces[0], sources[0])
    bounced, heard, middle, sent = pl.pallas_call(
        hand_on,
        out_shape=tuple(jax.ShapeDtypeStruct(r.shape, r.dtype) for r in results),
        in_specs=[pl.BlockSpec(memory_space=pl.ANY)] * 4,
        out_specs=[pl.BlockSpec(memory_space=pl.ANY)] * 4,
        scratch_shapes=[pltpu.VMEM(r.shape, r.dtype) for r in results]
        + [pltpu.SemaphoreType.DMA((4,)), pltpu.SemaphoreType.DMA((4,))],
        compiler_params=pltpu.CompilerParams(vmem_limit_bytes=VMEM),
    )(*results)
    return bounced[None], heard[None], middle[None], sent[None]


def solution(mesh):
    return jax.shard_map(
        shards,
        mesh=mesh,
        in_specs=(
            P("layer", "row", None),
            P("layer", "row", None),
            P("layer", "row", None),
            P("layer", "row", None),
            P("layer", "row", None),
            P("layer", None, "row", None),
        ),
        out_specs=(
            P("layer", None, "row", None),
            P("layer", None, "row", None),
            P("layer", None, "row", None),
            P("layer", "row", None),
        ),
        check_vma=False,
    )
```
